256 devices in a mesh: rx: 16 (over z, y_lo), ry: 4 (over x), ma: 4 (over y_hi, core).
Axes of the slice: x: 4, y: 4 (y_hi: 2, y_lo: 2; y = y_hi * 2 + y_lo), z: 8, core: 2. Of those that a mesh axis runs over, the one named last changes fastest.
Arguments:
- numerator: float32 [16, 4, 120, 13824], P('rx', 'ry', None, 'ma'), may hold values from -6 to 6
- weight: float32 [16, 4], P('rx', 'ry'), may hold values from 0.5 to 2
- inputs: bfloat16 [16, 4, 2, 256, 13824], P('rx', 'ry', None, None, 'ma'), may hold values from -0.125 to 0.125
- targets: float32 [16, 4, 2, 120, 256], P('rx', 'ry'), may hold values from -6 to 6
- first_moment: float32 [16, 4, 120, 13824], P('rx', 'ry', None, 'ma'), may hold values from -1.5 to 1.5
- second_moment: float32 [16, 4, 120, 13824], P('rx', 'ry', None, 'ma'), may hold values from 0.005 to 0.2
Outputs:
- new_numerator: float32 [16, 4, 120, 13824], P('rx', 'ry', None, 'ma')
- new_weight: float32 [16, 4], P('rx', 'ry')
- new_first: float32 [16, 4, 120, 13824], P('rx', 'ry', None, 'ma')
- new_second: float32 [16, 4, 120, 13824], P('rx', 'ry', None, 'ma')
The draws below stay inside these ranges and needn't reach their ends.
All inputs are finite; a program needn't handle non-finite values.
Results may differ from the reference program's by a relative error of at most 0.0003.
Values sent between devices are 32-bit elements; how exact they have to be, the bound alone decides.
No kernel may reach another device: no remote copies, remote signals or barrier semaphores. Data moves between devices by JAX's collectives and lax.ppermute only.
A program may use at most 64 MiB of HBM per device.

```python
import math
import jax
import jax.numpy as jnp
from jax import lax

FF = 13824
COLS = 120
TOK = 256
PRIOR_STEPS = 100
NRX = 16
NRY = 4


def steps_of(key, shape, split, least, top_value):
    factor_of, own = 1.0, jax.random.fold_in(key, 6)
    for dim, blocks in split:
        draws = jnp.exp(jax.random.uniform(jax.random.fold_in(own, dim), (blocks,), jnp.float32, least / len(split), top_value / len(split)))
        factor_of = factor_of * jnp.repeat(draws, shape[dim] // blocks).reshape([-1 if axis == dim else 1 for axis in range(len(shape))])
    return factor_of


def bell_draw(own_key, shape, deviation, limit, pieces=(), dtype=jnp.bfloat16):
    entries = jax.random.normal(own_key, shape, jnp.float32) * deviation
    if len(pieces) > 0:
        entries = steps_of(own_key, shape, pieces, -0.22, 0.18) * entries
    return jnp.clip(entries, min=-limit, max=limit).astype(dtype)


def setup_inputs(seed: int = 0) -> dict:
    splits = jax.random.split(jax.random.key(seed), 7)
    numerator = bell_draw(splits[0], (NRX, NRY, COLS, FF), 1.0, 6.0, ((0, 16), (1, 4), (3, 4)), jnp.float32)
    weight = jnp.clip(jnp.exp(math.log(2.0) - 1.3862944 * jax.random.uniform(splits[1], (NRX, NRY), jnp.float32) ** steps_of(splits[1], (NRX, NRY), ((0, 16), (1, 4)), -0.2, 0.2)), 0.5, 2.0)
    inputs = bell_draw(splits[2], (NRX, NRY, 2, TOK, FF), (FF // 6) ** -0.5, 0.125, ((0, 16), (1, 4), (4, 4)))
    targets = bell_draw(splits[3], (NRX, NRY, 2, COLS, TOK), 1.0, 6.0, ((0, 16), (1, 4)), jnp.float32)
    first_moment = bell_draw(splits[4], (NRX, NRY, COLS, FF), 0.1, 1.5, ((0, 16), (1, 4), (3, 4)), jnp.float32)
    second_moment = jnp.clip(jnp.exp(math.log(0.2) - 3.6888795 * jax.random.uniform(splits[5], (NRX, NRY, COLS, FF), jnp.float32) ** steps_of(splits[5], (NRX, NRY, COLS, FF), ((0, 16), (1, 4), (3, 4)), -0.2, 0.2)), 0.005, 0.2)
    return {"numerator": numerator, "weight": weight, "inputs": inputs, "targets": targets, "first_moment": first_moment, "second_moment": second_moment}


BETA_ONE = 0.9
BETA_TWO = 0.999
LEARN_RATE = 0.05
EPSILON = 1e-08

def gradient_of(packed):
    params, inputs_round, targets_round = packed
    inputs_wide = inputs_round.astype(jnp.float32)
    predicted = jnp.einsum('cf,tf->ct', params, inputs_wide, precision=lax.Precision.HIGHEST)
    residual = predicted - targets_round
    return jnp.einsum('ct,tf->cf', residual, inputs_wide, precision=lax.Precision.HIGHEST)

def adam_update(params, gradient, first, second, count):
    first = BETA_ONE * first + (1.0 - BETA_ONE) * gradient
    second = BETA_TWO * second + (1.0 - BETA_TWO) * gradient * gradient
    first_corr = 1.0 - BETA_ONE ** count
    second_corr = 1.0 - BETA_TWO ** count
    params = params - LEARN_RATE * (first / first_corr) / (jnp.sqrt(second / second_corr) + EPSILON)
    return (params, first, second)

def reference(numerator, weight, inputs, targets, first_moment, second_moment):
    values, scales = (numerator, weight)
    first, second = (first_moment, second_moment)
    for round_number in range(2):
        grid_axis = round_number
        values = (values + jnp.roll(values, 1, grid_axis) + jnp.roll(values, -1, grid_axis)) / 3.0
        scales = (scales + jnp.roll(scales, 1, grid_axis) + jnp.roll(scales, -1, grid_axis)) / 3.0
        params = values / scales[:, :, None, None]
        shape = params.shape
        flat_params = params.reshape((-1,) + shape[2:])
        flat_inputs = inputs[:, :, round_number].reshape((-1,) + inputs.shape[3:])
        flat_targets = targets[:, :, round_number].reshape((-1,) + targets.shape[3:])
        gradient = lax.map(gradient_of, (flat_params, flat_inputs, flat_targets)).reshape(shape)
        params, first, second = adam_update(params, gradient, first, second, PRIOR_STEPS + round_number + 1)
        values = scales[:, :, None, None] * params
    return (values, scales, first, second)
```

```python
import functools

import jax
import jax.numpy as jnp
from jax import lax
from jax.experimental import pallas as pl
from jax.experimental.pallas import tpu as pltpu
from jax.sharding import PartitionSpec as P

PRIOR_STEPS = 100
BETA_ONE = 0.9
BETA_TWO = 0.999
LEARN_RATE = 0.05
EPSILON = 1e-08

GROUPS = ((32, 32), (32, 24))
TILE = 384


def send(block, axis, target):
    return lax.ppermute(block, axis, [(i, target(i)) for i in range(lax.axis_size(axis))])


def partner(i):
    return i ^ 1


def outward(count, i):
    return (i + 2) % count if i % 2 == 0 else (i - 2) % count


def inward(count, i):
    return (i - 2) % count if i % 2 == 0 else (i + 2) % count


def in_vmem(block):
    return pltpu.with_memory_space_constraint(block, pltpu.VMEM)


def two_parts(block):
    high = block.astype(jnp.bfloat16).astype(jnp.float32)
    return jnp.concatenate([high, block - high], axis=0).astype(jnp.bfloat16)


def fold(block):
    half = block.shape[0] // 2
    return block[:half] + block[half:]


def tiles(width):
    return [(start, min(TILE, width - start)) for start in range(0, width, TILE)]


def predict_kernel(round_number, terms, n_rows, *refs):
    inputs_ref, *operands = refs[:-2]
    total_ref, pred_ref = refs[-2:]
    pred = jnp.zeros((n_rows, inputs_ref.shape[3]), jnp.float32)
    for start, width in tiles(total_ref.shape[1]):
        lanes = pl.ds(start, width)
        pieces = []
        for count, parts in terms:
            piece = None
            for which, row in parts:
                part = operands[which][pl.ds(row, count), lanes]
                piece = part if piece is None else piece + part
            pieces.append(piece)
        block = pieces[0] if len(pieces) == 1 else jnp.concatenate(pieces, axis=0)
        total_ref[:, lanes] = block
        product = lax.dot_general(
            two_parts(block),
            inputs_ref[0, 0, round_number, :, lanes],
            (((1,), (1,)), ((), ())),
            preferred_element_type=jnp.float32,
        )
        pred = pred + fold(product)
    pred_ref[...] = pred


def predict(round_number, inputs, operands, terms):
    n_rows = sum(count for count, _ in terms)
    width = operands[0].shape[-1]
    tokens = inputs.shape[3]
    vmem = pl.BlockSpec(memory_space=pltpu.VMEM)
    return pl.pallas_call(
        functools.partial(predict_kernel, round_number, terms, n_rows),
        in_specs=[vmem] * (1 + len(operands)),
        out_specs=[vmem, vmem],
        out_shape=[pltpu.VMEM((n_rows, width), jnp.float32), pltpu.VMEM((n_rows, tokens), jnp.float32)],
        compiler_params=pltpu.CompilerParams(vmem_limit_bytes=16 * 1024 * 1024),
        cost_estimate=pl.CostEstimate(
            flops=4 * n_rows * tokens * width, bytes_accessed=1 << 20, transcendentals=0
        ),
        name=f"predict{round_number}",
    )(in_vmem(inputs), *[in_vmem(block) for block in operands])


def adam_tile(count, gradient, first, second, params):
    first = BETA_ONE * first + (1.0 - BETA_ONE) * gradient
    second = BETA_TWO * second + (1.0 - BETA_TWO) * gradient * gradient
    first_corr = 1.0 - BETA_ONE**count
    second_corr = 1.0 - BETA_TWO**count
    step = (first * (LEARN_RATE / first_corr)) / (jnp.sqrt(second * (1.0 / second_corr)) + EPSILON)
    return params - step, first, second


def update_tiles(round_number, row, moment_row, n_rows, refs, store):
    inputs_ref, targets_ref, first_ref, second_ref, total_ref, mine_ref, other_ref, scale_ref = refs
    scale = scale_ref[0:1, 0:1]
    inverse = 1.0 / scale
    residual = (mine_ref[...] + other_ref[...]) * inverse - targets_ref[0, 0, round_number, pl.ds(row, n_rows), :]
    residual = two_parts(residual)
    for start, width in tiles(total_ref.shape[1]):
        lanes = pl.ds(start, width)
        gradient = fold(
            jnp.dot(residual, inputs_ref[0, 0, round_number, :, lanes], preferred_element_type=jnp.float32)
        )
        rows = pl.ds(moment_row, n_rows)
        params, first, second = adam_tile(
            PRIOR_STEPS + round_number + 1,
            gradient,
            first_ref[rows, lanes],
            second_ref[rows, lanes],
            total_ref[:, lanes] * inverse,
        )
        store(start, width, (params * (scale * (1.0 / 3.0)), first, second))


def middle_kernel(row, n_rows, *refs):
    values_ref, first_out, second_out = refs[-3:]

    def store(start, width, blocks):
        for ref, block in zip((values_ref, first_out, second_out), blocks):
            ref[:, pl.ds(start, width)] = block

    update_tiles(0, row, row, n_rows, refs[:-3], store)


def last_kernel(row, n_rows, n_aliased, *refs):
    outs = refs[8 + n_aliased : 11 + n_aliased]
    held, sems = refs[-2:]
    copies = []

    def store(start, width, blocks):
        lanes = pl.ds(start, width)
        for which, (ref, block) in enumerate(zip(outs, blocks)):
            held[which, :, lanes] = block
            copy = pltpu.make_async_copy(
                held.at[which, :, lanes],
                ref.at[0, 0, pl.ds(row, n_rows), lanes],
                sems.at[which, start // TILE],
            )
            copy.start()
            copies.append(copy)

    update_tiles(1, row, 0, n_rows, refs[:8], store)
    for copy in copies:
        copy.wait()


def update_cost(n_rows, tokens, width):
    return pl.CostEstimate(flops=4 * n_rows * tokens * width, bytes_accessed=1 << 20, transcendentals=n_rows * width)


def update_middle(row, n_rows, operands):
    width = operands[4].shape[-1]
    vmem = pl.BlockSpec(memory_space=pltpu.VMEM)
    return pl.pallas_call(
        functools.partial(middle_kernel, row, n_rows),
        in_specs=[vmem] * 8,
        out_specs=[vmem] * 3,
        out_shape=[pltpu.VMEM((n_rows, width), jnp.float32)] * 3,
        compiler_params=pltpu.CompilerParams(vmem_limit_bytes=16 * 1024 * 1024),
        cost_estimate=update_cost(n_rows, operands[0].shape[3], width),
        name="update0",
    )(*[in_vmem(block) for block in operands])


def update_last(row, n_rows, operands, whole_shape, previous):
    width = operands[4].shape[-1]
    vmem = pl.BlockSpec(memory_space=pltpu.VMEM)
    anywhere = pl.BlockSpec(memory_space=pltpu.HBM)
    return pl.pallas_call(
        functools.partial(last_kernel, row, n_rows, len(previous)),
        in_specs=[vmem] * 8 + [anywhere] * len(previous),
        out_specs=[anywhere] * 3,
        out_shape=[jax.ShapeDtypeStruct(whole_shape, jnp.float32)] * 3,
        scratch_shapes=[
            pltpu.VMEM((3, n_rows, width), jnp.float32),
            pltpu.SemaphoreType.DMA((3, len(tiles(width)))),
        ],
        input_output_aliases={8 + which: which for which in range(len(previous))},
        compiler_params=pltpu.CompilerParams(vmem_limit_bytes=24 * 1024 * 1024),
        cost_estimate=update_cost(n_rows, operands[0].shape[3], width),
        name="update1",
    )(*[in_vmem(block) for block in operands], *previous)


def summed_over_ma(pred):
    pair = pred + send(pred, "ma", lambda i: i ^ 1)
    return pair, send(pair, "ma", lambda i: i ^ 2)


def neighbours(block, axis):
    count = lax.axis_size(axis)
    return send(block, axis, lambda i: (i + 1) % count), send(block, axis, lambda i: (i - 1) % count)


def local(numerator, weight, inputs, targets, first_moment, second_moment):
    row_count = lax.axis_size("rx")
    own = numerator[0, 0]
    first = first_moment[0, 0]
    second = second_moment[0, 0]

    before, after = neighbours(weight, "ry")
    three = jnp.concatenate([weight, before, after], axis=1)
    left, right = neighbours(three, "rx")
    sums = three + left + right
    row_sum = sums[:, 0:1]
    column_sum = (sums[:, 0:1] + sums[:, 1:2] + sums[:, 2:3]) / 3.0
    new_weight = column_sum / 3.0

    out_of = functools.partial(outward, row_count)
    into = functools.partial(inward, row_count)
    starts = []
    row = 0
    for count_a, count_b in GROUPS:
        starts.append(row)
        row += count_a + count_b
    received = []
    for (count_a, count_b), row in zip(GROUPS, starts):
        mid, end = row + count_a, row + count_a + count_b
        across = send(own[row:mid], "rx", partner)
        further = send(across, "rx", out_of)
        along = send(own[mid:end], "rx", into)
        pair_sum = send(own[mid:end] + along, "rx", partner)
        received.append((across, further, pair_sum))

    outs = ()
    results = []
    for (count_a, count_b), row, (across, further, pair_sum) in zip(GROUPS, starts, received):
        n_rows = count_a + count_b
        terms = (
            (count_a, ((0, row), (1, 0), (2, 0))),
            (count_b, ((0, row + count_a), (3, 0))),
        )
        total, pred = predict(0, inputs, (own, across, further, pair_sum), terms)
        mine, other = summed_over_ma(pred)
        values, first_mid, second_mid = update_middle(
            row, n_rows, (inputs, targets, first, second, total, mine, other, row_sum)
        )
        before, after = neighbours(values, "ry")
        results.append((values, before, after, first_mid, second_mid))

    for (count_a, count_b), row, (values, before, after, first_mid, second_mid) in zip(GROUPS, starts, results):
        n_rows = count_a + count_b
        terms = ((n_rows, ((0, 0), (1, 0), (2, 0))),)
        total, pred = predict(1, inputs, (values, before, after), terms)
        mine, other = summed_over_ma(pred)
        outs = update_last(
            row,
            n_rows,
            (inputs, targets, first_mid, second_mid, total, mine, other, column_sum),
            numerator.shape,
            outs,
        )
    new_numerator, new_first, new_second = outs
    return new_numerator, new_weight, new_first, new_second


def solution(mesh):
    rows = P("rx", "ry", None, "ma")
    return jax.shard_map(
        local,
        mesh=mesh,
        in_specs=(
            rows,
            P("rx", "ry"),
            P("rx", "ry", None, None, "ma"),
            P("rx", "ry", None, None, None),
            rows,
            rows,
        ),
        out_specs=(rows, P("rx", "ry"), rows, rows),
        check_vma=False,
    )
```

```python
import functools

import jax
import jax.numpy as jnp
from jax import lax
from jax.experimental import pallas as pl
from jax.experimental.pallas import tpu as pltpu
from jax.sharding import PartitionSpec as P

PRIOR_STEPS = 100
BETA_ONE = 0.9
BETA_TWO = 0.999
LEARN_RATE = 0.05
EPSILON = 1e-08

GROUPS = ((32, 32), (24, 32))
BATCHES = ((0,), (1,))
TILE = 384
LANE_TILES = 27


def send(block, axis, target):
    return lax.ppermute(block, axis, [(i, target(i)) for i in range(lax.axis_size(axis))])


def partner(i):
    return i ^ 1


def outward(count, i):
    return (i + 2) % count if i % 2 == 0 else (i - 2) % count


def inward(count, i):
    return (i - 2) % count if i % 2 == 0 else (i + 2) % count


def after(block, *earlier):
    return lax.optimization_barrier((block, *earlier))[0]


def in_vmem(block):
    return pltpu.with_memory_space_constraint(block, pltpu.VMEM)


def two_parts(block):
    high = block.astype(jnp.bfloat16).astype(jnp.float32)
    return jnp.concatenate([high, block - high], axis=0).astype(jnp.bfloat16)


def fold(block):
    half = block.shape[0] // 2
    return block[:half] + block[half:]


def read(ref, row, count, start, width):
    if len(ref.shape) == 2:
        return ref[pl.ds(row, count), pl.ds(start, width)]
    lane_tiles = LANE_TILES
    rows = []
    for block in range(row // 8, (row + count) // 8):
        lanes = [ref[block * lane_tiles + lane] for lane in range(start // 128, (start + width) // 128)]
        rows.append(jnp.concatenate(lanes, axis=1))
    return jnp.concatenate(rows, axis=0)


def write(ref, row, start, block):
    count, width = block.shape
    if len(ref.shape) == 2:
        ref[pl.ds(row, count), pl.ds(start, width)] = block
        return
    for down in range(0, count, 8):
        for across in range(0, width, 128):
            tile = (row + down) // 8 * LANE_TILES + (start + across) // 128
            ref[tile] = block[down : down + 8, across : across + 128]


def packed_shape(n_rows):
    return (n_rows // 8 * LANE_TILES + 1, 8, 128)


def tiles(width):
    return [(start, min(TILE, width - start)) for start in range(0, width, TILE)]


def predict_kernel(round_number, terms, n_rows, scale_parts, *refs):
    n_out = 3 if scale_parts else 2
    inputs_ref, *operands = refs[:-n_out]
    total_ref, pred_ref = refs[-n_out:][:2]
    if scale_parts:
        scale = None
        for which in scale_parts:
            part = operands[which][operands[which].shape[0] - 1]
            scale = part if scale is None else scale + part
        refs[-1][...] = scale if round_number == 0 else scale * (1.0 / 3.0)
    pred = jnp.zeros((n_rows, inputs_ref.shape[3]), jnp.float32)
    for start, width in tiles(total_ref.shape[1]):
        pieces = []
        for count, parts in terms:
            piece = None
            for which, row in parts:
                part = read(operands[which], row, count, start, width)
                piece = part if piece is None else piece + part
            pieces.append(piece)
        block = pieces[0] if len(pieces) == 1 else jnp.concatenate(pieces, axis=0)
        total_ref[:, pl.ds(start, width)] = block
        product = lax.dot_general(
            two_parts(block),
            inputs_ref[0, 0, round_number, :, pl.ds(start, width)],
            (((1,), (1,)), ((), ())),
            preferred_element_type=jnp.float32,
        )
        pred = pred + fold(product)
    pred_ref[...] = pred


def predict(round_number, inputs, operands, terms, scale_parts):
    n_rows = sum(count for count, _ in terms)
    tokens, width = inputs.shape[3:]
    vmem = pl.BlockSpec(memory_space=pltpu.VMEM)
    shapes = [(n_rows, width), (n_rows, tokens)] + ([(8, 128)] if scale_parts else [])
    return pl.pallas_call(
        functools.partial(predict_kernel, round_number, terms, n_rows, scale_parts),
        in_specs=[vmem] * (1 + len(operands)),
        out_specs=[vmem] * len(shapes),
        out_shape=[pltpu.VMEM(shape, jnp.float32) for shape in shapes],
        compiler_params=pltpu.CompilerParams(vmem_limit_bytes=16 * 1024 * 1024),
        cost_estimate=pl.CostEstimate(
            flops=4 * n_rows * tokens * width, bytes_accessed=1 << 20, transcendentals=0
        ),
        name=f"predict{round_number}",
    )(in_vmem(inputs), *[in_vmem(block) for block in operands])


def adam_tile(count, gradient, first, second, params):
    first = BETA_ONE * first + (1.0 - BETA_ONE) * gradient
    second = BETA_TWO * second + (1.0 - BETA_TWO) * gradient * gradient
    first_corr = 1.0 - BETA_ONE**count
    second_corr = 1.0 - BETA_TWO**count
    step = (first * (LEARN_RATE / first_corr)) / (jnp.sqrt(second * (1.0 / second_corr)) + EPSILON)
    return params - step, first, second


def cut_kernel(row, counts, packed, numerator_ref, weight_ref, *refs):
    sems = refs[len(counts)]
    copies = []
    for which, count in enumerate(counts):
        target = refs[-1] if packed and which == 0 else refs[which]
        copy = pltpu.make_async_copy(numerator_ref.at[0, 0, pl.ds(row, count), :], target, sems.at[which])
        copy.start()
        copies.append(copy)
        row += count
    for copy in copies:
        copy.wait()
    if packed:
        for start, width in tiles(numerator_ref.shape[3]):
            write(refs[0], 0, start, refs[-1][:, pl.ds(start, width)])
        refs[0][refs[0].shape[0] - 1] = jnp.broadcast_to(weight_ref[...], (8, 128))


def cut(numerator, weight, row, counts, packed):
    width = numerator.shape[-1]
    vmem = pl.BlockSpec(memory_space=pltpu.VMEM)
    shapes = [(count, width) for count in counts]
    scratch = [pltpu.SemaphoreType.DMA((len(counts),))]
    if packed:
        shapes[0] = packed_shape(counts[0])
        scratch.append(pltpu.VMEM((counts[0], width), jnp.float32))
    return pl.pallas_call(
        functools.partial(cut_kernel, row, counts, packed),
        in_specs=[pl.BlockSpec(memory_space=pltpu.HBM), vmem],
        out_specs=[vmem] * len(counts),
        out_shape=[pltpu.VMEM(shape, jnp.float32) for shape in shapes],
        scratch_shapes=scratch,
        compiler_params=pltpu.CompilerParams(vmem_limit_bytes=4 * 1024 * 1024),
        cost_estimate=pl.CostEstimate(flops=0, bytes_accessed=1 << 20, transcendentals=0),
        name="cut",
    )(pltpu.with_memory_space_constraint(numerator, pltpu.HBM), weight)


def load_kernel(inputs_ref, held_ref, sem):
    copy = pltpu.make_async_copy(inputs_ref, held_ref, sem)
    copy.start()
    copy.wait()


def load(inputs):
    return pl.pallas_call(
        load_kernel,
        in_specs=[pl.BlockSpec(memory_space=pltpu.HBM)],
        out_specs=pl.BlockSpec(memory_space=pltpu.VMEM),
        out_shape=pltpu.VMEM(inputs.shape, inputs.dtype),
        scratch_shapes=[pltpu.SemaphoreType.DMA],
        compiler_params=pltpu.CompilerParams(vmem_limit_bytes=1024 * 1024),
        cost_estimate=pl.CostEstimate(flops=0, bytes_accessed=4 << 20, transcendentals=0),
        name="load",
    )(pltpu.with_memory_space_constraint(inputs, pltpu.HBM))


def update_tiles(round_number, row, pieces, refs, store):
    inputs_ref, targets_ref, total_ref, mine_ref, other_ref, scale_ref, *moments = refs
    n_rows, tokens = mine_ref.shape
    scale = jnp.concatenate([scale_ref[0:1, :]] * (TILE // 128), axis=1)
    inverse = 1.0 / scale
    scale = scale * (1.0 / 3.0)
    residual = (mine_ref[...] + other_ref[...]) * inverse[:, :tokens]
    residual = two_parts(residual - targets_ref[0, 0, round_number, pl.ds(row, n_rows), :])
    for start, width in tiles(total_ref.shape[1]):
        lanes = pl.ds(start, width)
        gradient = fold(
            jnp.dot(residual, inputs_ref[0, 0, round_number, :, lanes], preferred_element_type=jnp.float32)
        )
        done = 0
        for count, which, moment_row in pieces:
            rows = pl.ds(moment_row, count)
            params, first, second = adam_tile(
                PRIOR_STEPS + round_number + 1,
                gradient[done : done + count],
                moments[2 * which][rows, lanes],
                moments[2 * which + 1][rows, lanes],
                total_ref[pl.ds(done, count), lanes] * inverse[:, :width],
            )
            store(done, count, start, width, (params * scale[:, :width], first, second))
            done += count


def middle_kernel(row, pieces, n_operands, *refs):
    outs = refs[n_operands:]

    def store(done, count, start, width, blocks):
        for ref, block in zip(outs, blocks):
            write(ref, done, start, block)

    update_tiles(0, row, pieces, refs[:n_operands], store)
    if len(outs[0].shape) == 3:
        outs[0][outs[0].shape[0] - 1] = refs[5][...]


def last_kernel(row, pieces, n_operands, n_aliased, *refs):
    outs = refs[n_operands + n_aliased : n_operands + n_aliased + 3]
    weight_ref, held, sems = refs[-3:]
    copies = []
    weight_ref[...] = refs[5][0:1, 0:1] * (1.0 / 3.0)

    def store(done, count, start, width, blocks):
        lanes = pl.ds(start, width)
        for which, (ref, block) in enumerate(zip(outs, blocks)):
            held[which, pl.ds(done, count), lanes] = block
            copy = pltpu.make_async_copy(
                held.at[which, pl.ds(done, count), lanes],
                ref.at[0, 0, pl.ds(row + done, count), lanes],
                sems.at[len(copies)],
            )
            copy.start()
            copies.append(copy)

    update_tiles(1, row, pieces, refs[:n_operands], store)
    for copy in copies:
        copy.wait()


def update_cost(n_rows, tokens, width):
    return pl.CostEstimate(flops=4 * n_rows * tokens * width, bytes_accessed=1 << 20, transcendentals=n_rows * width)


def update_middle(row, operands, packed):
    n_rows, width = operands[2].shape
    vmem = pl.BlockSpec(memory_space=pltpu.VMEM)
    return pl.pallas_call(
        functools.partial(middle_kernel, row, ((n_rows, 0, row),), len(operands)),
        in_specs=[vmem] * len(operands),
        out_specs=[vmem] * 3,
        out_shape=[
            pltpu.VMEM(packed_shape(n_rows) if packed else (n_rows, width), jnp.float32),
            pltpu.VMEM((n_rows, width), jnp.float32),
            pltpu.VMEM((n_rows, width), jnp.float32),
        ],
        compiler_params=pltpu.CompilerParams(vmem_limit_bytes=16 * 1024 * 1024),
        cost_estimate=update_cost(n_rows, operands[0].shape[3], width),
        name="update0",
    )(*[in_vmem(block) for block in operands])


def update_last(row, pieces, operands, whole_shape, previous):
    n_rows, width = operands[2].shape
    vmem = pl.BlockSpec(memory_space=pltpu.VMEM)
    outer = pl.BlockSpec(memory_space=pltpu.HBM)
    return pl.pallas_call(
        functools.partial(last_kernel, row, pieces, len(operands), len(previous)),
        in_specs=[vmem] * len(operands) + [outer] * len(previous),
        out_specs=[outer] * 3 + [vmem],
        out_shape=[jax.ShapeDtypeStruct(whole_shape, jnp.float32)] * 3 + [jax.ShapeDtypeStruct((1, 1), jnp.float32)],
        scratch_shapes=[
            pltpu.VMEM((3, n_rows, width), jnp.float32),
            pltpu.SemaphoreType.DMA((3 * len(tiles(width)) * len(pieces),)),
        ],
        input_output_aliases={len(operands) + which: which for which in range(len(previous))},
        compiler_params=pltpu.CompilerParams(vmem_limit_bytes=24 * 1024 * 1024),
        cost_estimate=update_cost(n_rows, operands[0].shape[3], width),
        name="update1",
    )(*[in_vmem(block) for block in operands], *previous)


def summed_over_ma(pred):
    pair = pred + send(pred, "ma", lambda i: i ^ 1)
    return pair, send(pair, "ma", lambda i: i ^ 2)


def neighbours(block, axis):
    count = lax.axis_size(axis)
    return send(block, axis, lambda i: (i + 1) % count), send(block, axis, lambda i: (i - 1) % count)


def local(numerator, weight, inputs, targets, first_moment, second_moment):
    row_count = lax.axis_size("rx")
    first = first_moment[0, 0]
    second = second_moment[0, 0]
    out_of = functools.partial(outward, row_count)
    into = functools.partial(inward, row_count)
    own = []
    rows = []
    row = 0
    for group in GROUPS:
        own.append(cut(numerator, weight, row, group, row == 0))
        rows.append(row)
        row += sum(group)
    inputs = load(inputs)

    results = []
    across = send(own[0][0], "rx", partner)
    along = send(own[0][1], "rx", into)
    earlier = (inputs, own[1][0])
    for g, (own_a, own_b) in enumerate(own):
        pair_sum = after(own_b, *earlier) + along
        across_now = after(across, *earlier)
        if g + 1 < len(GROUPS):
            next_a, next_b = own[g + 1]
            along = send(after(next_b, pair_sum), "rx", into)
            across = send(after(next_a, pair_sum), "rx", partner)
        count_a, count_b = GROUPS[g]
        total, pred, *tile = predict(
            0,
            inputs,
            (own_a, across_now, send(across_now, "rx", out_of), own_b, send(pair_sum, "rx", partner)),
            ((count_a, ((0, 0), (1, 0), (2, 0))), (count_b, ((3, 0), (4, 0)))),
            (0, 1, 2) if g == 0 else (),
        )
        if g == 0:
            (row_sum,) = tile
        mine, other = summed_over_ma(pred)
        earlier = (other,)
        if g + 1 < len(GROUPS):
            total = after(total, along, across)
        values, first_mid, second_mid = update_middle(
            rows[g], (inputs, targets, total, mine, other, row_sum, first, second), g == 0
        )
        ready = after(values, *results[-1][1:3]) if g > 0 else values
        results.append((values, *neighbours(ready, "ry"), first_mid, second_mid))

    outs = ()
    for batch in BATCHES:
        operands = []
        terms = []
        for g in batch:
            values, before, next_one = results[g][:3]
            values = after(values, results[-1][0], *([other] if outs else []))
            terms.append((sum(GROUPS[g]), tuple((len(operands) + i, 0) for i in range(3))))
            operands += [values, before, next_one]
        total, pred, *tile = predict(1, inputs, tuple(operands), tuple(terms), (0, 1, 2) if not outs else ())
        if not outs:
            (column_sum,) = tile
        mine, other = summed_over_ma(pred)
        moments = [block for g in batch for block in results[g][3:]]
        outs = update_last(
            rows[batch[0]],
            tuple((sum(GROUPS[g]), which, 0) for which, g in enumerate(batch)),
            (inputs, targets, total, mine, other, column_sum, *moments),
            numerator.shape,
            outs[:3],
        )
    new_numerator, new_first, new_second, new_weight = outs
    return new_numerator, new_weight, new_first, new_second


def solution(mesh):
    rows = P("rx", "ry", None, "ma")
    return jax.shard_map(
        local,
        mesh=mesh,
        in_specs=(
            rows,
            P("rx", "ry"),
            P("rx", "ry", None, None, "ma"),
            P("rx", "ry", None, None, None),
            rows,
            rows,
        ),
        out_specs=(rows, P("rx", "ry"), rows, rows),
        check_vma=False,
    )
```

```python
import functools

import jax
import jax.numpy as jnp
from jax import lax
from jax.experimental import pallas as pl
from jax.experimental.pallas import tpu as pltpu
from jax.sharding import PartitionSpec as P

PRIOR_STEPS = 100
BETA_ONE = 0.9
BETA_TWO = 0.999
LEARN_RATE = 0.05
EPSILON = 1e-08

GROUPS = ((24, 24), (16, 24), (16, 16))
BATCHES = ((0, 1), (2,))
TILE = 384
COST = 120
RUN = 1152
LANE_TILES = 27


def send(block, axis, target):
    return lax.ppermute(block, axis, [(i, target(i)) for i in range(lax.axis_size(axis))])


def partner(i):
    return i ^ 1


def outward(count, i):
    return (i + 2) % count if i % 2 == 0 else (i - 2) % count


def inward(count, i):
    return (i - 2) % count if i % 2 == 0 else (i + 2) % count


def after(block, *earlier):
    return lax.optimization_barrier((block, *earlier))[0]


def in_vmem(block):
    return pltpu.with_memory_space_constraint(block, pltpu.VMEM)


def two_parts(block):
    high = block.astype(jnp.bfloat16).astype(jnp.float32)
    return jnp.concatenate([high, block - high], axis=0).astype(jnp.bfloat16)


def fold(block):
    half = block.shape[0] // 2
    return block[:half] + block[half:]


def read(ref, row, count, start, width):
    if len(ref.shape) == 2:
        return ref[pl.ds(row, count), pl.ds(start, width)]
    lane_tiles = LANE_TILES
    rows = []
    for block in range(row // 8, (row + count) // 8):
        lanes = [ref[block * lane_tiles + lane] for lane in range(start // 128, (start + width) // 128)]
        rows.append(jnp.concatenate(lanes, axis=1))
    return jnp.concatenate(rows, axis=0)


def write(ref, row, start, block):
    count, width = block.shape
    if len(ref.shape) == 2:
        ref[pl.ds(row, count), pl.ds(start, width)] = block
        return
    for down in range(0, count, 8):
        for across in range(0, width, 128):
            tile = (row + down) // 8 * LANE_TILES + (start + across) // 128
            ref[tile] = block[down : down + 8, across : across + 128]


def packed_shape(n_rows):
    return (n_rows // 8 * LANE_TILES + 1, 8, 128)


def tiles(width):
    return [(start, min(TILE, width - start)) for start in range(0, width, TILE)]


def predict_kernel(round_number, terms, n_rows, scale_parts, *refs):
    n_out = 3 if scale_parts else 2
    inputs_ref, *operands = refs[:-n_out]
    total_ref, pred_ref = refs[-n_out:][:2]
    if scale_parts:
        scale = None
        for which in scale_parts:
            part = operands[which][operands[which].shape[0] - 1]
            scale = part if scale is None else scale + part
        refs[-1][...] = scale if round_number == 0 else scale * (1.0 / 3.0)
    pred = jnp.zeros((n_rows, inputs_ref.shape[3]), jnp.float32)
    for start, width in tiles(total_ref.shape[1]):
        pieces = []
        for count, parts in terms:
            piece = None
            for which, row in parts:
                part = read(operands[which], row, count, start, width)
                piece = part if piece is None else piece + part
            pieces.append(piece)
        block = pieces[0] if len(pieces) == 1 else jnp.concatenate(pieces, axis=0)
        total_ref[:, pl.ds(start, width)] = block
        product = lax.dot_general(
            two_parts(block),
            inputs_ref[0, 0, round_number, :, pl.ds(start, width)],
            (((1,), (1,)), ((), ())),
            preferred_element_type=jnp.float32,
        )
        pred = pred + fold(product)
    pred_ref[...] = pred


def predict(round_number, inputs, operands, terms, scale_parts):
    n_rows = sum(count for count, _ in terms)
    tokens, width = inputs.shape[3:]
    vmem = pl.BlockSpec(memory_space=pltpu.VMEM)
    shapes = [(n_rows, width), (n_rows, tokens)] + ([(8, 128)] if scale_parts else [])
    return pl.pallas_call(
        functools.partial(predict_kernel, round_number, terms, n_rows, scale_parts),
        in_specs=[vmem] * (1 + len(operands)),
        out_specs=[vmem] * len(shapes),
        out_shape=[pltpu.VMEM(shape, jnp.float32) for shape in shapes],
        compiler_params=pltpu.CompilerParams(vmem_limit_bytes=16 * 1024 * 1024),
        cost_estimate=pl.CostEstimate(
            flops=4 * n_rows * tokens * width, bytes_accessed=1 << 20, transcendentals=0
        ),
        name=f"predict{round_number}",
    )(in_vmem(inputs), *[in_vmem(block) for block in operands])


def adam_tile(count, gradient, first, second, params):
    first = BETA_ONE * first + (1.0 - BETA_ONE) * gradient
    second = BETA_TWO * second + (1.0 - BETA_TWO) * gradient * gradient
    first_corr = 1.0 - BETA_ONE**count
    second_corr = 1.0 - BETA_TWO**count
    step = (first * (LEARN_RATE / first_corr)) / (jnp.sqrt(second * (1.0 / second_corr)) + EPSILON)
    return params - step, first, second


def cut_kernel(row, counts, packed, numerator_ref, weight_ref, *refs):
    sems = refs[len(counts)]
    copies = []
    for which, count in enumerate(counts):
        target = refs[-1] if packed and which == 0 else refs[which]
        copy = pltpu.make_async_copy(numerator_ref.at[0, 0, pl.ds(row, count), :], target, sems.at[which])
        copy.start()
        copies.append(copy)
        row += count
    for copy in copies:
        copy.wait()
    if packed:
        for start, width in tiles(numerator_ref.shape[3]):
            write(refs[0], 0, start, refs[-1][:, pl.ds(start, width)])
        refs[0][refs[0].shape[0] - 1] = jnp.broadcast_to(weight_ref[...], (8, 128))


def cut(numerator, weight, row, counts, packed):
    width = numerator.shape[-1]
    vmem = pl.BlockSpec(memory_space=pltpu.VMEM)
    shapes = [(count, width) for count in counts]
    scratch = [pltpu.SemaphoreType.DMA((len(counts),))]
    if packed:
        shapes[0] = packed_shape(counts[0])
        scratch.append(pltpu.VMEM((counts[0], width), jnp.float32))
    return pl.pallas_call(
        functools.partial(cut_kernel, row, counts, packed),
        in_specs=[pl.BlockSpec(memory_space=pltpu.HBM), vmem],
        out_specs=[vmem] * len(counts),
        out_shape=[pltpu.VMEM(shape, jnp.float32) for shape in shapes],
        scratch_shapes=scratch,
        compiler_params=pltpu.CompilerParams(vmem_limit_bytes=4 * 1024 * 1024),
        cost_estimate=pl.CostEstimate(flops=0, bytes_accessed=1 << 20, transcendentals=0),
        name="cut",
    )(pltpu.with_memory_space_constraint(numerator, pltpu.HBM), weight)


def load_kernel(inputs_ref, held_ref, sem):
    copy = pltpu.make_async_copy(inputs_ref, held_ref, sem)
    copy.start()
    copy.wait()


def load(inputs):
    return pl.pallas_call(
        load_kernel,
        in_specs=[pl.BlockSpec(memory_space=pltpu.HBM)],
        out_specs=pl.BlockSpec(memory_space=pltpu.VMEM),
        out_shape=pltpu.VMEM(inputs.shape, inputs.dtype),
        scratch_shapes=[pltpu.SemaphoreType.DMA],
        compiler_params=pltpu.CompilerParams(vmem_limit_bytes=1024 * 1024),
        cost_estimate=pl.CostEstimate(flops=0, bytes_accessed=4 << 20, transcendentals=0),
        name="load",
    )(pltpu.with_memory_space_constraint(inputs, pltpu.HBM))


def update_tiles(round_number, row, pieces, refs, store):
    inputs_ref, targets_ref, total_ref, mine_ref, other_ref, scale_ref, *moments = refs
    n_rows, tokens = mine_ref.shape
    scale = jnp.concatenate([scale_ref[0:1, :]] * (TILE // 128), axis=1)
    inverse = 1.0 / scale
    scale = scale * (1.0 / 3.0)
    residual = (mine_ref[...] + other_ref[...]) * inverse[:, :tokens]
    residual = two_parts(residual - targets_ref[0, 0, round_number, pl.ds(row, n_rows), :])
    for start, width in tiles(total_ref.shape[1]):
        lanes = pl.ds(start, width)
        gradient = fold(
            jnp.dot(residual, inputs_ref[0, 0, round_number, :, lanes], preferred_element_type=jnp.float32)
        )
        done = 0
        for count, which, moment_row in pieces:
            rows = pl.ds(moment_row, count)
            params, first, second = adam_tile(
                PRIOR_STEPS + round_number + 1,
                gradient[done : done + count],
                moments[2 * which][rows, lanes],
                moments[2 * which + 1][rows, lanes],
                total_ref[pl.ds(done, count), lanes] * inverse[:, :width],
            )
            store(done, count, start, width, (params * scale[:, :width], first, second))
            done += count


def middle_kernel(row, pieces, n_operands, *refs):
    outs = refs[n_operands:]

    def store(done, count, start, width, blocks):
        for ref, block in zip(outs, blocks):
            write(ref, done, start, block)

    update_tiles(0, row, pieces, refs[:n_operands], store)
    if len(outs[0].shape) == 3:
        outs[0][outs[0].shape[0] - 1] = refs[5][...]


def last_kernel(row, pieces, n_operands, n_aliased, *refs):
    outs = refs[n_operands + n_aliased : n_operands + n_aliased + 3]
    weight_ref, held, sems = refs[-3:]
    n_rows, width = held.shape[1:]
    copies = []
    weight_ref[...] = refs[5][0:1, 0:1] * (1.0 / 3.0)

    def store(done, count, start, size, blocks):
        for which, block in enumerate(blocks):
            held[which, pl.ds(done, count), pl.ds(start, size)] = block
        if done + count < n_rows or (start + size) % RUN != 0:
            return
        lanes = pl.ds(start + size - RUN, RUN)
        for which, ref in enumerate(outs):
            copy = pltpu.make_async_copy(
                held.at[which, :, lanes],
                ref.at[0, 0, pl.ds(row, n_rows), lanes],
                sems.at[len(copies)],
            )
            copy.start()
            copies.append(copy)

    update_tiles(1, row, pieces, refs[:n_operands], store)
    for copy in copies:
        copy.wait()


def update_cost(n_rows, tokens, width):
    return pl.CostEstimate(flops=COST * n_rows * tokens * width, bytes_accessed=1 << 20, transcendentals=n_rows * width)


def update_middle(row, operands, packed):
    n_rows, width = operands[2].shape
    vmem = pl.BlockSpec(memory_space=pltpu.VMEM)
    return pl.pallas_call(
        functools.partial(middle_kernel, row, ((n_rows, 0, row),), len(operands)),
        in_specs=[vmem] * len(operands),
        out_specs=[vmem] * 3,
        out_shape=[
            pltpu.VMEM(packed_shape(n_rows) if packed else (n_rows, width), jnp.float32),
            pltpu.VMEM((n_rows, width), jnp.float32),
            pltpu.VMEM((n_rows, width), jnp.float32),
        ],
        compiler_params=pltpu.CompilerParams(vmem_limit_bytes=16 * 1024 * 1024),
        cost_estimate=update_cost(n_rows, operands[0].shape[3], width),
        name="update0",
    )(*[in_vmem(block) for block in operands])


def update_last(row, pieces, operands, whole_shape, previous):
    n_rows, width = operands[2].shape
    vmem = pl.BlockSpec(memory_space=pltpu.VMEM)
    outer = pl.BlockSpec(memory_space=pltpu.HBM)
    return pl.pallas_call(
        functools.partial(last_kernel, row, pieces, len(operands), len(previous)),
        in_specs=[vmem] * len(operands) + [outer] * len(previous),
        out_specs=[outer] * 3 + [vmem],
        out_shape=[jax.ShapeDtypeStruct(whole_shape, jnp.float32)] * 3 + [jax.ShapeDtypeStruct((1, 1), jnp.float32)],
        scratch_shapes=[
            pltpu.VMEM((3, n_rows, width), jnp.float32),
            pltpu.SemaphoreType.DMA((3 * width // RUN,)),
        ],
        input_output_aliases={len(operands) + which: which for which in range(len(previous))},
        compiler_params=pltpu.CompilerParams(vmem_limit_bytes=24 * 1024 * 1024),
        cost_estimate=update_cost(n_rows, operands[0].shape[3], width),
        name="update1",
    )(*[in_vmem(block) for block in operands], *previous)


def summed_over_ma(pred):
    pair = pred + send(pred, "ma", lambda i: i ^ 1)
    return pair, send(pair, "ma", lambda i: i ^ 2)


def neighbours(block, axis):
    count = lax.axis_size(axis)
    return send(block, axis, lambda i: (i + 1) % count), send(block, axis, lambda i: (i - 1) % count)


def local(numerator, weight, inputs, targets, first_moment, second_moment):
    row_count = lax.axis_size("rx")
    first = first_moment[0, 0]
    second = second_moment[0, 0]
    out_of = functools.partial(outward, row_count)
    into = functools.partial(inward, row_count)
    own = []
    rows = []
    row = 0
    for group in GROUPS:
        pieces = cut(numerator, weight, row, [count for count in group if count > 0], row == 0)
        own.append(pieces if group[0] > 0 else (None, *pieces))
        rows.append(row)
        row += sum(group)
    inputs = load(inputs)

    results = []
    across = send(own[0][0], "rx", partner)
    along = send(own[0][1], "rx", into)
    earlier = (inputs, *[group[1] for group in own[1:]])
    for g, (own_a, own_b) in enumerate(own):
        if g > 0:
            earlier = (mine,) if across is None else (across, mine)
        pair_sum = after(own_b, *earlier) + along
        summed = send(pair_sum, "rx", partner)
        count_a, count_b = GROUPS[g]
        operands = (own_b, summed)
        terms = ((count_b, ((0, 0), (1, 0))),)
        if own_a is not None:
            across_now = after(across, pair_sum)
            operands += (own_a, across_now, send(across_now, "rx", out_of))
            terms = ((count_a, ((2, 0), (3, 0), (4, 0))), *terms)
        if g + 1 < len(GROUPS):
            next_a, next_b = own[g + 1]
            along = send(after(next_b, pair_sum), "rx", into)
            across = None if next_a is None else send(after(next_a, summed), "rx", partner)
        total, pred, *tile = predict(0, inputs, operands, terms, (2, 3, 4) if g == 0 else ())
        if g == 0:
            (row_sum,) = tile
        mine, other = summed_over_ma(pred)
        if g + 1 < len(GROUPS):
            total = after(total, along, *([] if across is None else [across]))
        values, first_mid, second_mid = update_middle(
            rows[g], (inputs, targets, total, mine, other, row_sum, first, second), g == 0
        )
        ready = after(values, *results[-1][1:3]) if g > 0 else values
        results.append((values, *neighbours(ready, "ry"), first_mid, second_mid))

    outs = ()
    for batch in BATCHES:
        operands = []
        terms = []
        for g in batch:
            values, before, next_one = results[g][:3]
            values = after(values, results[-1][0], *([other] if outs else []))
            terms.append((sum(GROUPS[g]), tuple((len(operands) + i, 0) for i in range(3))))
            operands += [values, before, next_one]
        total, pred, *tile = predict(1, inputs, tuple(operands), tuple(terms), (0, 1, 2) if not outs else ())
        if not outs:
            (column_sum,) = tile
        mine, other = summed_over_ma(pred)
        moments = [block for g in batch for block in results[g][3:]]
        outs = update_last(
            rows[batch[0]],
            tuple((sum(GROUPS[g]), which, 0) for which, g in enumerate(batch)),
            (inputs, targets, total, mine, other, column_sum, *moments),
            numerator.shape,
            outs[:3],
        )
    new_numerator, new_first, new_second, new_weight = outs
    return new_numerator, new_weight, new_first, new_second


def solution(mesh):
    rows = P("rx", "ry", None, "ma")
    return jax.shard_map(
        local,
        mesh=mesh,
        in_specs=(
            rows,
            P("rx", "ry"),
            P("rx", "ry", None, None, "ma"),
            P("rx", "ry", None, None, None),
            rows,
            rows,
        ),
        out_specs=(rows, P("rx", "ry"), rows, rows),
        check_vma=False,
    )
```

```python
import functools

import jax
import jax.numpy as jnp
from jax import lax
from jax.experimental import pallas as pl
from jax.experimental.pallas import tpu as pltpu
from jax.sharding import PartitionSpec as P

PRIOR_STEPS = 100
BETA_ONE = 0.9
BETA_TWO = 0.999
LEARN_RATE = 0.05
EPSILON = 1e-08

GROUPS = ((24, 24), (16, 24), (16, 16))
BATCHES = ((0, 1), (2,))
TILE = 384
COST = 120
RUN = 1152
LANE_TILES = 27


def send(block, axis, target):
    return lax.ppermute(block, axis, [(i, target(i)) for i in range(lax.axis_size(axis))])


def partner(i):
    return i ^ 1


def outward(count, i):
    return (i + 2) % count if i % 2 == 0 else (i - 2) % count


def inward(count, i):
    return (i - 2) % count if i % 2 == 0 else (i + 2) % count


def after(block, *earlier):
    return lax.optimization_barrier((block, *earlier))[0]


def in_vmem(block):
    return pltpu.with_memory_space_constraint(block, pltpu.VMEM)


def two_parts(block):
    high = block.astype(jnp.bfloat16).astype(jnp.float32)
    return jnp.concatenate([high, block - high], axis=0).astype(jnp.bfloat16)


def fold(block):
    half = block.shape[0] // 2
    return block[:half] + block[half:]


def read(ref, row, count, start, width):
    if len(ref.shape) == 2:
        return ref[pl.ds(row, count), pl.ds(start, width)]
    lane_tiles = LANE_TILES
    rows = []
    for block in range(row // 8, (row + count) // 8):
        lanes = [ref[block * lane_tiles + lane] for lane in range(start // 128, (start + width) // 128)]
        rows.append(jnp.concatenate(lanes, axis=1))
    return jnp.concatenate(rows, axis=0)


def write(ref, row, start, block):
    count, width = block.shape
    if len(ref.shape) == 2:
        ref[pl.ds(row, count), pl.ds(start, width)] = block
        return
    for down in range(0, count, 8):
        for across in range(0, width, 128):
            tile = (row + down) // 8 * LANE_TILES + (start + across) // 128
            ref[tile] = block[down : down + 8, across : across + 128]


def packed_shape(n_rows):
    return (n_rows // 8 * LANE_TILES + 1, 8, 128)


def tiles(width):
    return [(start, min(TILE, width - start)) for start in range(0, width, TILE)]


def predict_kernel(round_number, terms, n_rows, scale_parts, *refs):
    n_out = 3 if scale_parts else 2
    inputs_ref, *operands = refs[:-n_out]
    total_ref, pred_ref = refs[-n_out:][:2]
    if scale_parts:
        scale = None
        for which in scale_parts:
            part = operands[which][operands[which].shape[0] - 1]
            scale = part if scale is None else scale + part
        refs[-1][...] = scale if round_number == 0 else scale * (1.0 / 3.0)
    pred = jnp.zeros((n_rows, inputs_ref.shape[3]), jnp.float32)
    for start, width in tiles(total_ref.shape[1]):
        pieces = []
        for count, parts in terms:
            piece = None
            for which, row in parts:
                part = read(operands[which], row, count, start, width)
                piece = part if piece is None else piece + part
            pieces.append(piece)
        block = pieces[0] if len(pieces) == 1 else jnp.concatenate(pieces, axis=0)
        total_ref[:, pl.ds(start, width)] = block
        product = lax.dot_general(
            two_parts(block),
            inputs_ref[0, 0, round_number, :, pl.ds(start, width)],
            (((1,), (1,)), ((), ())),
            preferred_element_type=jnp.float32,
        )
        pred = pred + fold(product)
    pred_ref[...] = pred


def predict(round_number, inputs, operands, terms, scale_parts):
    n_rows = sum(count for count, _ in terms)
    tokens, width = inputs.shape[3:]
    vmem = pl.BlockSpec(memory_space=pltpu.VMEM)
    shapes = [(n_rows, width), (n_rows, tokens)] + ([(8, 128)] if scale_parts else [])
    return pl.pallas_call(
        functools.partial(predict_kernel, round_number, terms, n_rows, scale_parts),
        in_specs=[vmem] * (1 + len(operands)),
        out_specs=[vmem] * len(shapes),
        out_shape=[pltpu.VMEM(shape, jnp.float32) for shape in shapes],
        compiler_params=pltpu.CompilerParams(vmem_limit_bytes=16 * 1024 * 1024),
        cost_estimate=pl.CostEstimate(
            flops=4 * n_rows * tokens * width, bytes_accessed=1 << 20, transcendentals=0
        ),
        name=f"predict{round_number}",
    )(in_vmem(inputs), *[in_vmem(block) for block in operands])


def adam_tile(count, gradient, first, second, params):
    first = BETA_ONE * first + (1.0 - BETA_ONE) * gradient
    second = BETA_TWO * second + (1.0 - BETA_TWO) * gradient * gradient
    first_corr = 1.0 - BETA_ONE**count
    second_corr = 1.0 - BETA_TWO**count
    step = (first * (LEARN_RATE / first_corr)) / (jnp.sqrt(second * (1.0 / second_corr)) + EPSILON)
    return params - step, first, second


def cut_kernel(row, counts, packed, numerator_ref, weight_ref, *refs):
    sems = refs[len(counts)]
    copies = []
    for which, count in enumerate(counts):
        target = refs[-1] if packed and which == 0 else refs[which]
        copy = pltpu.make_async_copy(numerator_ref.at[0, 0, pl.ds(row, count), :], target, sems.at[which])
        copy.start()
        copies.append(copy)
        row += count
    for copy in copies:
        copy.wait()
    if packed:
        for start, width in tiles(numerator_ref.shape[3]):
            write(refs[0], 0, start, refs[-1][:, pl.ds(start, width)])
        refs[0][refs[0].shape[0] - 1] = jnp.broadcast_to(weight_ref[...], (8, 128))


def cut(numerator, weight, row, counts, packed):
    width = numerator.shape[-1]
    vmem = pl.BlockSpec(memory_space=pltpu.VMEM)
    shapes = [(count, width) for count in counts]
    scratch = [pltpu.SemaphoreType.DMA((len(counts),))]
    if packed:
        shapes[0] = packed_shape(counts[0])
        scratch.append(pltpu.VMEM((counts[0], width), jnp.float32))
    return pl.pallas_call(
        functools.partial(cut_kernel, row, counts, packed),
        in_specs=[pl.BlockSpec(memory_space=pltpu.HBM), vmem],
        out_specs=[vmem] * len(counts),
        out_shape=[pltpu.VMEM(shape, jnp.float32) for shape in shapes],
        scratch_shapes=scratch,
        compiler_params=pltpu.CompilerParams(vmem_limit_bytes=4 * 1024 * 1024),
        cost_estimate=pl.CostEstimate(flops=0, bytes_accessed=1 << 20, transcendentals=0),
        name="cut",
    )(pltpu.with_memory_space_constraint(numerator, pltpu.HBM), weight)


def load_kernel(inputs_ref, held_ref, sem):
    copy = pltpu.make_async_copy(inputs_ref, held_ref, sem)
    copy.start()
    copy.wait()


def load(inputs):
    return pl.pallas_call(
        load_kernel,
        in_specs=[pl.BlockSpec(memory_space=pltpu.HBM)],
        out_specs=pl.BlockSpec(memory_space=pltpu.VMEM),
        out_shape=pltpu.VMEM(inputs.shape, inputs.dtype),
        scratch_shapes=[pltpu.SemaphoreType.DMA],
        compiler_params=pltpu.CompilerParams(vmem_limit_bytes=1024 * 1024),
        cost_estimate=pl.CostEstimate(flops=0, bytes_accessed=4 << 20, transcendentals=0),
        name="load",
    )(pltpu.with_memory_space_constraint(inputs, pltpu.HBM))


def update_tiles(round_number, row, pieces, refs, store):
    inputs_ref, targets_ref, total_ref, scale_ref, *rest = refs
    moments, preds = rest[: 2 * len(pieces)], rest[2 * len(pieces) :]
    n_rows, tokens = preds[0].shape
    predicted = preds[0][...]
    for ref in preds[1:]:
        predicted = predicted + ref[...]
    scale = jnp.concatenate([scale_ref[0:1, :]] * (TILE // 128), axis=1)
    inverse = 1.0 / scale
    scale = scale * (1.0 / 3.0)
    residual = predicted * inverse[:, :tokens]
    residual = two_parts(residual - targets_ref[0, 0, round_number, pl.ds(row, n_rows), :])
    for start, width in tiles(total_ref.shape[1]):
        lanes = pl.ds(start, width)
        gradient = fold(
            jnp.dot(residual, inputs_ref[0, 0, round_number, :, lanes], preferred_element_type=jnp.float32)
        )
        done = 0
        for count, which, moment_row in pieces:
            rows = pl.ds(moment_row, count)
            params, first, second = adam_tile(
                PRIOR_STEPS + round_number + 1,
                gradient[done : done + count],
                moments[2 * which][rows, lanes],
                moments[2 * which + 1][rows, lanes],
                total_ref[pl.ds(done, count), lanes] * inverse[:, :width],
            )
            store(done, count, start, width, (params * scale[:, :width], first, second))
            done += count


def middle_kernel(row, pieces, n_operands, *refs):
    outs = refs[n_operands:]

    def store(done, count, start, width, blocks):
        for ref, block in zip(outs, blocks):
            write(ref, done, start, block)

    update_tiles(0, row, pieces, refs[:n_operands], store)
    if len(outs[0].shape) == 3:
        outs[0][outs[0].shape[0] - 1] = refs[3][...]


def last_kernel(row, pieces, n_operands, n_aliased, *refs):
    outs = refs[n_operands + n_aliased : n_operands + n_aliased + 3]
    weight_ref, held, sems = refs[-3:]
    n_rows, width = held.shape[1:]
    copies = []
    weight_ref[...] = refs[3][0:1, 0:1] * (1.0 / 3.0)

    def store(done, count, start, size, blocks):
        for which, block in enumerate(blocks):
            held[which, pl.ds(done, count), pl.ds(start, size)] = block
        if done + count < n_rows or (start + size) % RUN != 0:
            return
        lanes = pl.ds(start + size - RUN, RUN)
        for which, ref in enumerate(outs):
            copy = pltpu.make_async_copy(
                held.at[which, :, lanes],
                ref.at[0, 0, pl.ds(row, n_rows), lanes],
                sems.at[len(copies)],
            )
            copy.start()
            copies.append(copy)

    update_tiles(1, row, pieces, refs[:n_operands], store)
    for copy in copies:
        copy.wait()


def update_cost(n_rows, tokens, width):
    return pl.CostEstimate(flops=COST * n_rows * tokens * width, bytes_accessed=1 << 20, transcendentals=n_rows * width)


def update_middle(row, operands, packed):
    n_rows, width = operands[2].shape
    vmem = pl.BlockSpec(memory_space=pltpu.VMEM)
    return pl.pallas_call(
        functools.partial(middle_kernel, row, ((n_rows, 0, row),), len(operands)),
        in_specs=[vmem] * len(operands),
        out_specs=[vmem] * 3,
        out_shape=[
            pltpu.VMEM(packed_shape(n_rows) if packed else (n_rows, width), jnp.float32),
            pltpu.VMEM((n_rows, width), jnp.float32),
            pltpu.VMEM((n_rows, width), jnp.float32),
        ],
        compiler_params=pltpu.CompilerParams(vmem_limit_bytes=16 * 1024 * 1024),
        cost_estimate=update_cost(n_rows, operands[0].shape[3], width),
        name="update0",
    )(*[in_vmem(block) for block in operands])


def update_last(row, pieces, operands, whole_shape, previous):
    n_rows, width = operands[2].shape
    vmem = pl.BlockSpec(memory_space=pltpu.VMEM)
    outer = pl.BlockSpec(memory_space=pltpu.HBM)
    return pl.pallas_call(
        functools.partial(last_kernel, row, pieces, len(operands), len(previous)),
        in_specs=[vmem] * len(operands) + [outer] * len(previous),
        out_specs=[outer] * 3 + [vmem],
        out_shape=[jax.ShapeDtypeStruct(whole_shape, jnp.float32)] * 3 + [jax.ShapeDtypeStruct((1, 1), jnp.float32)],
        scratch_shapes=[
            pltpu.VMEM((3, n_rows, width), jnp.float32),
            pltpu.SemaphoreType.DMA((3 * width // RUN,)),
        ],
        input_output_aliases={len(operands) + which: which for which in range(len(previous))},
        compiler_params=pltpu.CompilerParams(vmem_limit_bytes=24 * 1024 * 1024),
        cost_estimate=update_cost(n_rows, operands[0].shape[3], width),
        name="update1",
    )(*[in_vmem(block) for block in operands], *previous)


def summed_over_ma(pred):
    pair = pred + send(pred, "ma", lambda i: i ^ 1)
    return pair, send(pair, "ma", lambda i: i ^ 2)


def gathered_over_ma(pred):
    return (pred, *[send(pred, "ma", functools.partial(lambda turn, i: i ^ turn, turn)) for turn in (3, 2, 1)])


def neighbours(block, axis):
    count = lax.axis_size(axis)
    return send(block, axis, lambda i: (i + 1) % count), send(block, axis, lambda i: (i - 1) % count)


def local(numerator, weight, inputs, targets, first_moment, second_moment):
    row_count = lax.axis_size("rx")
    first = first_moment[0, 0]
    second = second_moment[0, 0]
    out_of = functools.partial(outward, row_count)
    into = functools.partial(inward, row_count)
    own = []
    rows = []
    row = 0
    for group in GROUPS:
        pieces = cut(numerator, weight, row, [count for count in group if count > 0], row == 0)
        own.append(pieces if group[0] > 0 else (None, *pieces))
        rows.append(row)
        row += sum(group)
    inputs = load(inputs)

    results = []
    across = send(own[0][0], "rx", partner)
    along = send(own[0][1], "rx", into)
    earlier = (inputs, *[group[1] for group in own[1:]])
    for g, (own_a, own_b) in enumerate(own):
        if g > 0:
            earlier = (mine,) if across is None else (across, mine)
        pair_sum = after(own_b, *earlier) + along
        summed = send(pair_sum, "rx", partner)
        count_a, count_b = GROUPS[g]
        operands = (own_b, summed)
        terms = ((count_b, ((0, 0), (1, 0))),)
        if own_a is not None:
            across_now = after(across, pair_sum)
            operands += (own_a, across_now, send(across_now, "rx", out_of))
            terms = ((count_a, ((2, 0), (3, 0), (4, 0))), *terms)
        if g + 1 < len(GROUPS):
            next_a, next_b = own[g + 1]
            along = send(after(next_b, pair_sum), "rx", into)
            across = None if next_a is None else send(after(next_a, summed), "rx", partner)
        total, pred, *tile = predict(0, inputs, operands, terms, (2, 3, 4) if g == 0 else ())
        if g == 0:
            (row_sum,) = tile
        mine, other = summed_over_ma(pred)
        if g + 1 < len(GROUPS):
            total = after(total, along, *([] if across is None else [across]))
        values, first_mid, second_mid = update_middle(
            rows[g], (inputs, targets, total, row_sum, first, second, mine, other), g == 0
        )
        ready = after(values, *results[-1][1:3]) if g > 0 else values
        results.append((values, *neighbours(ready, "ry"), first_mid, second_mid))

    outs = ()
    for batch in BATCHES:
        operands = []
        terms = []
        for g in batch:
            values, before, next_one = results[g][:3]
            values = after(values, results[-1][0], *([other] if outs else []))
            terms.append((sum(GROUPS[g]), tuple((len(operands) + i, 0) for i in range(3))))
            operands += [values, before, next_one]
        total, pred, *tile = predict(1, inputs, tuple(operands), tuple(terms), (0, 1, 2) if not outs else ())
        if not outs:
            (column_sum,) = tile
        preds = gathered_over_ma(pred) if outs else summed_over_ma(pred)
        other = preds[-1]
        moments = [block for g in batch for block in results[g][3:]]
        outs = update_last(
            rows[batch[0]],
            tuple((sum(GROUPS[g]), which, 0) for which, g in enumerate(batch)),
            (inputs, targets, total, column_sum, *moments, *preds),
            numerator.shape,
            outs[:3],
        )
    new_numerator, new_first, new_second, new_weight = outs
    return new_numerator, new_weight, new_first, new_second


def solution(mesh):
    rows = P("rx", "ry", None, "ma")
    return jax.shard_map(
        local,
        mesh=mesh,
        in_specs=(
            rows,
            P("rx", "ry"),
            P("rx", "ry", None, None, "ma"),
            P("rx", "ry", None, None, None),
            rows,
            rows,
        ),
        out_specs=(rows, P("rx", "ry"), rows, rows),
        check_vma=False,
    )
```

```python
import functools

import jax
import jax.numpy as jnp
from jax import lax
from jax.experimental import pallas as pl
from jax.experimental.pallas import tpu as pltpu
from jax.sharding import PartitionSpec as P

PRIOR_STEPS = 100
BETA_ONE = 0.9
BETA_TWO = 0.999
LEARN_RATE = 0.05
EPSILON = 1e-08

GROUPS = ((24, 24), (16, 24), (16, 16))
BATCHES = ((0, 1), (2,))
TILE = 384
COST = 120
RUN = 1152
LANE_TILES = 27


def send(block, axis, target):
    return lax.ppermute(block, axis, [(i, target(i)) for i in range(lax.axis_size(axis))])


def partner(i):
    return i ^ 1


def outward(count, i):
    return (i + 2) % count if i % 2 == 0 else (i - 2) % count


def inward(count, i):
    return (i - 2) % count if i % 2 == 0 else (i + 2) % count


def after(block, *earlier):
    return lax.optimization_barrier((block, *earlier))[0]


def in_vmem(block):
    return pltpu.with_memory_space_constraint(block, pltpu.VMEM)


def two_parts(block):
    high = block.astype(jnp.bfloat16).astype(jnp.float32)
    return jnp.concatenate([high, block - high], axis=0).astype(jnp.bfloat16)


def fold(block):
    half = block.shape[0] // 2
    return block[:half] + block[half:]


def read(ref, row, count, start, width):
    if len(ref.shape) == 2:
        return ref[pl.ds(row, count), pl.ds(start, width)]
    lane_tiles = LANE_TILES
    rows = []
    for block in range(row // 8, (row + count) // 8):
        lanes = [ref[block * lane_tiles + lane] for lane in range(start // 128, (start + width) // 128)]
        rows.append(jnp.concatenate(lanes, axis=1))
    return jnp.concatenate(rows, axis=0)


def write(ref, row, start, block):
    count, width = block.shape
    if len(ref.shape) == 2:
        ref[pl.ds(row, count), pl.ds(start, width)] = block
        return
    for down in range(0, count, 8):
        for across in range(0, width, 128):
            tile = (row + down) // 8 * LANE_TILES + (start + across) // 128
            ref[tile] = block[down : down + 8, across : across + 128]


def packed_shape(n_rows):
    return (n_rows // 8 * LANE_TILES + 1, 8, 128)


def tiles(width):
    return [(start, min(TILE, width - start)) for start in range(0, width, TILE)]


def predict_kernel(round_number, terms, n_rows, scale_parts, *refs):
    n_out = 3 if scale_parts else 2
    inputs_ref, *operands = refs[:-n_out]
    total_ref, pred_ref = refs[-n_out:][:2]
    if scale_parts:
        scale = None
        for which in scale_parts:
            part = operands[which][operands[which].shape[0] - 1]
            scale = part if scale is None else scale + part
        refs[-1][...] = scale if round_number == 0 else scale * (1.0 / 3.0)
    pred = jnp.zeros((n_rows, inputs_ref.shape[3]), jnp.float32)
    for start, width in tiles(total_ref.shape[1]):
        pieces = []
        for count, parts in terms:
            piece = None
            for which, row in parts:
                part = read(operands[which], row, count, start, width)
                piece = part if piece is None else piece + part
            pieces.append(piece)
        block = pieces[0] if len(pieces) == 1 else jnp.concatenate(pieces, axis=0)
        total_ref[:, pl.ds(start, width)] = block
        product = lax.dot_general(
            two_parts(block),
            inputs_ref[0, 0, round_number, :, pl.ds(start, width)],
            (((1,), (1,)), ((), ())),
            preferred_element_type=jnp.float32,
        )
        pred = pred + fold(product)
    pred_ref[...] = pred


def predict(round_number, inputs, operands, terms, scale_parts):
    n_rows = sum(count for count, _ in terms)
    tokens, width = inputs.shape[3:]
    vmem = pl.BlockSpec(memory_space=pltpu.VMEM)
    shapes = [(n_rows, width), (n_rows, tokens)] + ([(8, 128)] if scale_parts else [])
    return pl.pallas_call(
        functools.partial(predict_kernel, round_number, terms, n_rows, scale_parts),
        in_specs=[vmem] * (1 + len(operands)),
        out_specs=[vmem] * len(shapes),
        out_shape=[pltpu.VMEM(shape, jnp.float32) for shape in shapes],
        compiler_params=pltpu.CompilerParams(vmem_limit_bytes=16 * 1024 * 1024),
        cost_estimate=pl.CostEstimate(
            flops=4 * n_rows * tokens * width, bytes_accessed=1 << 20, transcendentals=0
        ),
        name=f"predict{round_number}",
    )(in_vmem(inputs), *[in_vmem(block) for block in operands])


def adam_tile(count, gradient, first, second, params):
    first = BETA_ONE * first + (1.0 - BETA_ONE) * gradient
    second = BETA_TWO * second + (1.0 - BETA_TWO) * gradient * gradient
    first_corr = 1.0 - BETA_ONE**count
    second_corr = 1.0 - BETA_TWO**count
    step = (first * (LEARN_RATE / first_corr)) / (jnp.sqrt(second * (1.0 / second_corr)) + EPSILON)
    return params - step, first, second


def cut_kernel(row, counts, packed, numerator_ref, weight_ref, *refs):
    sems = refs[len(counts)]
    copies = []
    for which, count in enumerate(counts):
        target = refs[-1] if packed and which == 0 else refs[which]
        copy = pltpu.make_async_copy(numerator_ref.at[0, 0, pl.ds(row, count), :], target, sems.at[which])
        copy.start()
        copies.append(copy)
        row += count
    for copy in copies:
        copy.wait()
    if packed:
        for start, width in tiles(numerator_ref.shape[3]):
            write(refs[0], 0, start, refs[-1][:, pl.ds(start, width)])
        refs[0][refs[0].shape[0] - 1] = jnp.broadcast_to(weight_ref[...], (8, 128))


def cut(numerator, weight, row, counts, packed):
    width = numerator.shape[-1]
    vmem = pl.BlockSpec(memory_space=pltpu.VMEM)
    shapes = [(count, width) for count in counts]
    scratch = [pltpu.SemaphoreType.DMA((len(counts),))]
    if packed:
        shapes[0] = packed_shape(counts[0])
        scratch.append(pltpu.VMEM((counts[0], width), jnp.float32))
    return pl.pallas_call(
        functools.partial(cut_kernel, row, counts, packed),
        in_specs=[pl.BlockSpec(memory_space=pltpu.HBM), vmem],
        out_specs=[vmem] * len(counts),
        out_shape=[pltpu.VMEM(shape, jnp.float32) for shape in shapes],
        scratch_shapes=scratch,
        compiler_params=pltpu.CompilerParams(vmem_limit_bytes=4 * 1024 * 1024),
        cost_estimate=pl.CostEstimate(flops=0, bytes_accessed=1 << 20, transcendentals=0),
        name="cut",
    )(pltpu.with_memory_space_constraint(numerator, pltpu.HBM), weight)


def load_kernel(inputs_ref, held_ref, sem):
    copy = pltpu.make_async_copy(inputs_ref, held_ref, sem)
    copy.start()
    copy.wait()


def load(inputs):
    return pl.pallas_call(
        load_kernel,
        in_specs=[pl.BlockSpec(memory_space=pltpu.HBM)],
        out_specs=pl.BlockSpec(memory_space=pltpu.VMEM),
        out_shape=pltpu.VMEM(inputs.shape, inputs.dtype),
        scratch_shapes=[pltpu.SemaphoreType.DMA],
        compiler_params=pltpu.CompilerParams(vmem_limit_bytes=1024 * 1024),
        cost_estimate=pl.CostEstimate(flops=0, bytes_accessed=4 << 20, transcendentals=0),
        name="load",
    )(pltpu.with_memory_space_constraint(inputs, pltpu.HBM))


def update_tiles(round_number, row, pieces, refs, store):
    inputs_ref, targets_ref, total_ref, scale_ref, *rest = refs
    moments, preds = rest[: 2 * len(pieces)], rest[2 * len(pieces) :]
    n_rows, tokens = preds[0].shape
    predicted = preds[0][...]
    for ref in preds[1:]:
        predicted = predicted + ref[...]
    scale = jnp.concatenate([scale_ref[0:1, :]] * (TILE // 128), axis=1)
    inverse = 1.0 / scale
    scale = scale * (1.0 / 3.0)
    residual = predicted * inverse[:, :tokens]
    residual = two_parts(residual - targets_ref[0, 0, round_number, pl.ds(row, n_rows), :])
    for start, width in tiles(total_ref.shape[1]):
        lanes = pl.ds(start, width)
        gradient = fold(
            jnp.dot(residual, inputs_ref[0, 0, round_number, :, lanes], preferred_element_type=jnp.float32)
        )
        done = 0
        for count, which, moment_row in pieces:
            rows = pl.ds(moment_row, count)
            params, first, second = adam_tile(
                PRIOR_STEPS + round_number + 1,
                gradient[done : done + count],
                moments[2 * which][rows, lanes],
                moments[2 * which + 1][rows, lanes],
                total_ref[pl.ds(done, count), lanes] * inverse[:, :width],
            )
            store(done, count, start, width, (params * scale[:, :width], first, second))
            done += count


def middle_kernel(row, pieces, n_operands, *refs):
    outs = refs[n_operands:]

    def store(done, count, start, width, blocks):
        for ref, block in zip(outs, blocks):
            write(ref, done, start, block)

    update_tiles(0, row, pieces, refs[:n_operands], store)
    if len(outs[0].shape) == 3:
        outs[0][outs[0].shape[0] - 1] = refs[3][...]


def last_kernel(row, pieces, n_operands, n_aliased, *refs):
    outs = refs[n_operands + n_aliased : n_operands + n_aliased + 3]
    weight_ref, held, sems = refs[-3:]
    n_rows, width = held.shape[1:]
    copies = []
    weight_ref[...] = refs[3][0:1, 0:1] * (1.0 / 3.0)

    def store(done, count, start, size, blocks):
        for which, block in enumerate(blocks):
            held[which, pl.ds(done, count), pl.ds(start, size)] = block
        if done + count < n_rows or (start + size) % RUN != 0:
            return
        lanes = pl.ds(start + size - RUN, RUN)
        for which, ref in enumerate(outs):
            copy = pltpu.make_async_copy(
                held.at[which, :, lanes],
                ref.at[0, 0, pl.ds(row, n_rows), lanes],
                sems.at[len(copies)],
            )
            copy.start()
            copies.append(copy)

    update_tiles(1, row, pieces, refs[:n_operands], store)
    for copy in copies:
        copy.wait()


def update_cost(n_rows, tokens, width):
    return pl.CostEstimate(flops=COST * n_rows * tokens * width, bytes_accessed=1 << 20, transcendentals=n_rows * width)


def update_middle(row, operands, packed):
    n_rows, width = operands[2].shape
    vmem = pl.BlockSpec(memory_space=pltpu.VMEM)
    return pl.pallas_call(
        functools.partial(middle_kernel, row, ((n_rows, 0, row),), len(operands)),
        in_specs=[vmem] * len(operands),
        out_specs=[vmem] * 3,
        out_shape=[
            pltpu.VMEM(packed_shape(n_rows) if packed else (n_rows, width), jnp.float32),
            pltpu.VMEM((n_rows, width), jnp.float32),
            pltpu.VMEM((n_rows, width), jnp.float32),
        ],
        compiler_params=pltpu.CompilerParams(vmem_limit_bytes=16 * 1024 * 1024),
        cost_estimate=update_cost(n_rows, operands[0].shape[3], width),
        name="update0",
    )(*[in_vmem(block) for block in operands])


def update_last(row, pieces, operands, whole_shape, previous):
    n_rows, width = operands[2].shape
    vmem = pl.BlockSpec(memory_space=pltpu.VMEM)
    outer = pl.BlockSpec(memory_space=pltpu.HBM)
    return pl.pallas_call(
        functools.partial(last_kernel, row, pieces, len(operands), len(previous)),
        in_specs=[vmem] * len(operands) + [outer] * len(previous),
        out_specs=[outer] * 3 + [vmem],
        out_shape=[jax.ShapeDtypeStruct(whole_shape, jnp.float32)] * 3 + [jax.ShapeDtypeStruct((1, 1), jnp.float32)],
        scratch_shapes=[
            pltpu.VMEM((3, n_rows, width), jnp.float32),
            pltpu.SemaphoreType.DMA((3 * width // RUN,)),
        ],
        input_output_aliases={len(operands) + which: which for which in range(len(previous))},
        compiler_params=pltpu.CompilerParams(vmem_limit_bytes=24 * 1024 * 1024),
        cost_estimate=update_cost(n_rows, operands[0].shape[3], width),
        name="update1",
    )(*[in_vmem(block) for block in operands], *previous)


def summed_over_ma(pred):
    pair = pred + send(pred, "ma", lambda i: i ^ 1)
    return pair, send(pair, "ma", lambda i: i ^ 2)


def gathered_over_ma(pred):
    return (pred, *[send(pred, "ma", functools.partial(lambda turn, i: i ^ turn, turn)) for turn in (3, 2, 1)])


def upward(i):
    return (i + 1) % lax.axis_size("ry")


def downward(i):
    return (i - 1) % lax.axis_size("ry")


def local(numerator, weight, inputs, targets, first_moment, second_moment):
    row_count = lax.axis_size("rx")
    first = first_moment[0, 0]
    second = second_moment[0, 0]
    out_of = functools.partial(outward, row_count)
    into = functools.partial(inward, row_count)
    own = []
    rows = []
    row = 0
    for group in GROUPS:
        pieces = cut(numerator, weight, row, [count for count in group if count > 0], row == 0)
        own.append(pieces if group[0] > 0 else (None, *pieces))
        rows.append(row)
        row += sum(group)
    inputs = load(inputs)

    results = []
    across = send(own[0][0], "rx", partner)
    along = send(own[0][1], "rx", into)
    earlier = (inputs, *[group[1] for group in own[1:]])
    for g, (own_a, own_b) in enumerate(own):
        if g > 0:
            earlier = (mine,) if across is None else (across, mine)
        pair_sum = after(own_b, *earlier) + along
        summed = send(pair_sum, "rx", partner)
        count_a, count_b = GROUPS[g]
        operands = (own_b, summed)
        terms = ((count_b, ((0, 0), (1, 0))),)
        if own_a is not None:
            across_now = after(across, pair_sum)
            operands += (own_a, across_now, send(across_now, "rx", out_of))
            terms = ((count_a, ((2, 0), (3, 0), (4, 0))), *terms)
        if g + 1 < len(GROUPS):
            next_a, next_b = own[g + 1]
            along = send(after(next_b, pair_sum), "rx", into)
            across = None if next_a is None else send(after(next_a, summed), "rx", partner)
        total, pred, *tile = predict(0, inputs, operands, terms, (2, 3, 4) if g == 0 else ())
        if g == 0:
            (row_sum,) = tile
        mine, other = summed_over_ma(pred)
        if g + 1 < len(GROUPS):
            total = after(total, along, *([] if across is None else [across]))
        values, first_mid, second_mid = update_middle(
            rows[g], (inputs, targets, total, row_sum, first, second, mine, other), g == 0
        )
        came = [after(values, earlier_one) for earlier_one in results[-1][1:3]] if g > 0 else [values] * 2
        sides = (send(block, "ry", turn) for block, turn in zip(came, (upward, downward)))
        results.append((values, *sides, first_mid, second_mid))

    outs = ()
    for batch in BATCHES:
        operands = []
        terms = []
        for g in batch:
            values, before, next_one = results[g][:3]
            values = after(values, results[-1][0], *([other] if outs else []))
            terms.append((sum(GROUPS[g]), tuple((len(operands) + i, 0) for i in range(3))))
            operands += [values, before, next_one]
        total, pred, *tile = predict(1, inputs, tuple(operands), tuple(terms), (0, 1, 2) if not outs else ())
        if not outs:
            (column_sum,) = tile
        preds = gathered_over_ma(pred) if outs else summed_over_ma(pred)
        other = preds[-1]
        moments = [block for g in batch for block in results[g][3:]]
        outs = update_last(
            rows[batch[0]],
            tuple((sum(GROUPS[g]), which, 0) for which, g in enumerate(batch)),
            (inputs, targets, total, column_sum, *moments, *preds),
            numerator.shape,
            outs[:3],
        )
    new_numerator, new_first, new_second, new_weight = outs
    return new_numerator, new_weight, new_first, new_second


def solution(mesh):
    rows = P("rx", "ry", None, "ma")
    return jax.shard_map(
        local,
        mesh=mesh,
        in_specs=(
            rows,
            P("rx", "ry"),
            P("rx", "ry", None, None, "ma"),
            P("rx", "ry", None, None, None),
            rows,
            rows,
        ),
        out_specs=(rows, P("rx", "ry"), rows, rows),
        check_vma=False,
    )
```

```python
import functools

import jax
import jax.numpy as jnp
from jax import lax
from jax.experimental import pallas as pl
from jax.experimental.pallas import tpu as pltpu
from jax.sharding import PartitionSpec as P

PRIOR_STEPS = 100
BETA_ONE = 0.9
BETA_TWO = 0.999
LEARN_RATE = 0.05
EPSILON = 1e-08

GROUPS = ((24, 24), (16, 24), (16, 16))
BATCHES = ((0,), (1, 2))
TILE = 384
COST = 120
RUN = 1152
LANE_TILES = 27


def send(block, axis, target):
    return lax.ppermute(block, axis, [(i, target(i)) for i in range(lax.axis_size(axis))])


def partner(i):
    return i ^ 1


def outward(count, i):
    return (i + 2) % count if i % 2 == 0 else (i - 2) % count


def inward(count, i):
    return (i - 2) % count if i % 2 == 0 else (i + 2) % count


def after(block, *earlier):
    return lax.optimization_barrier((block, *earlier))[0]


def in_vmem(block):
    return pltpu.with_memory_space_constraint(block, pltpu.VMEM)


def two_parts(block):
    high = block.astype(jnp.bfloat16).astype(jnp.float32)
    return jnp.concatenate([high, block - high], axis=0).astype(jnp.bfloat16)


def fold(block):
    half = block.shape[0] // 2
    return block[:half] + block[half:]


def read(ref, row, count, start, width):
    if len(ref.shape) == 2:
        return ref[pl.ds(row, count), pl.ds(start, width)]
    lane_tiles = LANE_TILES
    rows = []
    for block in range(row // 8, (row + count) // 8):
        lanes = [ref[block * lane_tiles + lane] for lane in range(start // 128, (start + width) // 128)]
        rows.append(jnp.concatenate(lanes, axis=1))
    return jnp.concatenate(rows, axis=0)


def write(ref, row, start, block):
    count, width = block.shape
    if len(ref.shape) == 2:
        ref[pl.ds(row, count), pl.ds(start, width)] = block
        return
    for down in range(0, count, 8):
        for across in range(0, width, 128):
            tile = (row + down) // 8 * LANE_TILES + (start + across) // 128
            ref[tile] = block[down : down + 8, across : across + 128]


def packed_shape(n_rows):
    return (n_rows // 8 * LANE_TILES + 1, 8, 128)


def tiles(width):
    return [(start, min(TILE, width - start)) for start in range(0, width, TILE)]


def predict_kernel(round_number, terms, n_rows, scale_parts, *refs):
    n_out = 3 if scale_parts else 2
    inputs_ref, *operands = refs[:-n_out]
    total_ref, pred_ref = refs[-n_out:][:2]
    if scale_parts:
        scale = None
        for which in scale_parts:
            part = operands[which][operands[which].shape[0] - 1]
            scale = part if scale is None else scale + part
        refs[-1][...] = scale if round_number == 0 else scale * (1.0 / 3.0)
    pred = jnp.zeros((n_rows, inputs_ref.shape[3]), jnp.float32)
    for start, width in tiles(total_ref.shape[1]):
        pieces = []
        for count, parts in terms:
            piece = None
            for which, row in parts:
                part = read(operands[which], row, count, start, width)
                piece = part if piece is None else piece + part
            pieces.append(piece)
        block = pieces[0] if len(pieces) == 1 else jnp.concatenate(pieces, axis=0)
        total_ref[:, pl.ds(start, width)] = block
        product = lax.dot_general(
            two_parts(block),
            inputs_ref[0, 0, round_number, :, pl.ds(start, width)],
            (((1,), (1,)), ((), ())),
            preferred_element_type=jnp.float32,
        )
        pred = pred + fold(product)
    pred_ref[...] = pred


def predict(round_number, inputs, operands, terms, scale_parts):
    n_rows = sum(count for count, _ in terms)
    tokens, width = inputs.shape[3:]
    vmem = pl.BlockSpec(memory_space=pltpu.VMEM)
    shapes = [(n_rows, width), (n_rows, tokens)] + ([(8, 128)] if scale_parts else [])
    return pl.pallas_call(
        functools.partial(predict_kernel, round_number, terms, n_rows, scale_parts),
        in_specs=[vmem] * (1 + len(operands)),
        out_specs=[vmem] * len(shapes),
        out_shape=[pltpu.VMEM(shape, jnp.float32) for shape in shapes],
        compiler_params=pltpu.CompilerParams(vmem_limit_bytes=16 * 1024 * 1024),
        cost_estimate=pl.CostEstimate(
            flops=4 * n_rows * tokens * width, bytes_accessed=1 << 20, transcendentals=0
        ),
        name=f"predict{round_number}",
    )(in_vmem(inputs), *[in_vmem(block) for block in operands])


def adam_tile(count, gradient, first, second, params):
    first = BETA_ONE * first + (1.0 - BETA_ONE) * gradient
    second = BETA_TWO * second + (1.0 - BETA_TWO) * gradient * gradient
    first_corr = 1.0 - BETA_ONE**count
    second_corr = 1.0 - BETA_TWO**count
    step = (first * (LEARN_RATE / first_corr)) / (jnp.sqrt(second * (1.0 / second_corr)) + EPSILON)
    return params - step, first, second


def cut_kernel(row, counts, packed, numerator_ref, weight_ref, *refs):
    sems = refs[len(counts)]
    copies = []
    for which, count in enumerate(counts):
        target = refs[-1] if packed and which == 0 else refs[which]
        copy = pltpu.make_async_copy(numerator_ref.at[0, 0, pl.ds(row, count), :], target, sems.at[which])
        copy.start()
        copies.append(copy)
        row += count
    for copy in copies:
        copy.wait()
    if packed:
        for start, width in tiles(numerator_ref.shape[3]):
            write(refs[0], 0, start, refs[-1][:, pl.ds(start, width)])
        refs[0][refs[0].shape[0] - 1] = jnp.broadcast_to(weight_ref[...], (8, 128))


def cut(numerator, weight, row, counts, packed):
    width = numerator.shape[-1]
    vmem = pl.BlockSpec(memory_space=pltpu.VMEM)
    shapes = [(count, width) for count in counts]
    scratch = [pltpu.SemaphoreType.DMA((len(counts),))]
    if packed:
        shapes[0] = packed_shape(counts[0])
        scratch.append(pltpu.VMEM((counts[0], width), jnp.float32))
    return pl.pallas_call(
        functools.partial(cut_kernel, row, counts, packed),
        in_specs=[pl.BlockSpec(memory_space=pltpu.HBM), vmem],
        out_specs=[vmem] * len(counts),
        out_shape=[pltpu.VMEM(shape, jnp.float32) for shape in shapes],
        scratch_shapes=scratch,
        compiler_params=pltpu.CompilerParams(vmem_limit_bytes=4 * 1024 * 1024),
        cost_estimate=pl.CostEstimate(flops=0, bytes_accessed=1 << 20, transcendentals=0),
        name="cut",
    )(pltpu.with_memory_space_constraint(numerator, pltpu.HBM), weight)


def load_kernel(inputs_ref, held_ref, sem):
    copy = pltpu.make_async_copy(inputs_ref, held_ref, sem)
    copy.start()
    copy.wait()


def load(inputs):
    return pl.pallas_call(
        load_kernel,
        in_specs=[pl.BlockSpec(memory_space=pltpu.HBM)],
        out_specs=pl.BlockSpec(memory_space=pltpu.VMEM),
        out_shape=pltpu.VMEM(inputs.shape, inputs.dtype),
        scratch_shapes=[pltpu.SemaphoreType.DMA],
        compiler_params=pltpu.CompilerParams(vmem_limit_bytes=1024 * 1024),
        cost_estimate=pl.CostEstimate(flops=0, bytes_accessed=4 << 20, transcendentals=0),
        name="load",
    )(pltpu.with_memory_space_constraint(inputs, pltpu.HBM))


def update_tiles(round_number, row, pieces, refs, store):
    inputs_ref, targets_ref, total_ref, mine_ref, other_ref, scale_ref, *moments = refs
    n_rows, tokens = mine_ref.shape
    scale = jnp.concatenate([scale_ref[0:1, :]] * (TILE // 128), axis=1)
    inverse = 1.0 / scale
    scale = scale * (1.0 / 3.0)
    residual = (mine_ref[...] + other_ref[...]) * inverse[:, :tokens]
    residual = two_parts(residual - targets_ref[0, 0, round_number, pl.ds(row, n_rows), :])
    for start, width in tiles(total_ref.shape[1]):
        lanes = pl.ds(start, width)
        gradient = fold(
            jnp.dot(residual, inputs_ref[0, 0, round_number, :, lanes], preferred_element_type=jnp.float32)
        )
        done = 0
        for count, which, moment_row in pieces:
            rows = pl.ds(moment_row, count)
            params, first, second = adam_tile(
                PRIOR_STEPS + round_number + 1,
                gradient[done : done + count],
                moments[2 * which][rows, lanes],
                moments[2 * which + 1][rows, lanes],
                total_ref[pl.ds(done, count), lanes] * inverse[:, :width],
            )
            store(done, count, start, width, (params * scale[:, :width], first, second))
            done += count


def middle_kernel(row, pieces, n_operands, *refs):
    outs = refs[n_operands:]

    def store(done, count, start, width, blocks):
        for ref, block in zip(outs, blocks):
            write(ref, done, start, block)

    update_tiles(0, row, pieces, refs[:n_operands], store)
    if len(outs[0].shape) == 3:
        outs[0][outs[0].shape[0] - 1] = refs[5][...]


def last_kernel(row, pieces, n_operands, n_aliased, *refs):
    outs = refs[n_operands + n_aliased : n_operands + n_aliased + 3]
    weight_ref, held, sems = refs[-3:]
    n_rows, width = held.shape[1:]
    copies = []
    weight_ref[...] = refs[5][0:1, 0:1] * (1.0 / 3.0)

    def store(done, count, start, size, blocks):
        for which, block in enumerate(blocks):
            held[which, pl.ds(done, count), pl.ds(start, size)] = block
        if done + count < n_rows or (start + size) % RUN != 0:
            return
        lanes = pl.ds(start + size - RUN, RUN)
        for which, ref in enumerate(outs):
            copy = pltpu.make_async_copy(
                held.at[which, :, lanes],
                ref.at[0, 0, pl.ds(row, n_rows), lanes],
                sems.at[len(copies)],
            )
            copy.start()
            copies.append(copy)

    update_tiles(1, row, pieces, refs[:n_operands], store)
    for copy in copies:
        copy.wait()


def update_cost(n_rows, tokens, width):
    return pl.CostEstimate(flops=COST * n_rows * tokens * width, bytes_accessed=1 << 20, transcendentals=n_rows * width)


def update_middle(row, operands, packed):
    n_rows, width = operands[2].shape
    vmem = pl.BlockSpec(memory_space=pltpu.VMEM)
    return pl.pallas_call(
        functools.partial(middle_kernel, row, ((n_rows, 0, row),), len(operands)),
        in_specs=[vmem] * len(operands),
        out_specs=[vmem] * 3,
        out_shape=[
            pltpu.VMEM(packed_shape(n_rows) if packed else (n_rows, width), jnp.float32),
            pltpu.VMEM((n_rows, width), jnp.float32),
            pltpu.VMEM((n_rows, width), jnp.float32),
        ],
        compiler_params=pltpu.CompilerParams(vmem_limit_bytes=16 * 1024 * 1024),
        cost_estimate=update_cost(n_rows, operands[0].shape[3], width),
        name="update0",
    )(*[in_vmem(block) for block in operands])


def update_last(row, pieces, operands, whole_shape, previous):
    n_rows, width = operands[2].shape
    vmem = pl.BlockSpec(memory_space=pltpu.VMEM)
    outer = pl.BlockSpec(memory_space=pltpu.HBM)
    return pl.pallas_call(
        functools.partial(last_kernel, row, pieces, len(operands), len(previous)),
        in_specs=[vmem] * len(operands) + [outer] * len(previous),
        out_specs=[outer] * 3 + [vmem],
        out_shape=[jax.ShapeDtypeStruct(whole_shape, jnp.float32)] * 3 + [jax.ShapeDtypeStruct((1, 1), jnp.float32)],
        scratch_shapes=[
            pltpu.VMEM((3, n_rows, width), jnp.float32),
            pltpu.SemaphoreType.DMA((3 * width // RUN,)),
        ],
        input_output_aliases={len(operands) + which: which for which in range(len(previous))},
        compiler_params=pltpu.CompilerParams(vmem_limit_bytes=24 * 1024 * 1024),
        cost_estimate=update_cost(n_rows, operands[0].shape[3], width),
        name="update1",
    )(*[in_vmem(block) for block in operands], *previous)


def summed_over_ma(pred):
    pair = pred + send(pred, "ma", lambda i: i ^ 1)
    return pair, send(pair, "ma", lambda i: i ^ 2)


def neighbours(block, axis):
    count = lax.axis_size(axis)
    return send(block, axis, lambda i: (i + 1) % count), send(block, axis, lambda i: (i - 1) % count)


def local(numerator, weight, inputs, targets, first_moment, second_moment):
    row_count = lax.axis_size("rx")
    first = first_moment[0, 0]
    second = second_moment[0, 0]
    out_of = functools.partial(outward, row_count)
    into = functools.partial(inward, row_count)
    own = []
    rows = []
    row = 0
    for group in GROUPS:
        pieces = cut(numerator, weight, row, [count for count in group if count > 0], row == 0)
        own.append(pieces if group[0] > 0 else (None, *pieces))
        rows.append(row)
        row += sum(group)
    inputs = load(inputs)

    results = []
    across = send(own[0][0], "rx", partner)
    along = send(own[0][1], "rx", into)
    earlier = (inputs, *[group[1] for group in own[1:]])
    for g, (own_a, own_b) in enumerate(own):
        if g > 0:
            earlier = (mine,) if across is None else (across, mine)
        pair_sum = after(own_b, *earlier) + along
        summed = send(pair_sum, "rx", partner)
        count_a, count_b = GROUPS[g]
        operands = (own_b, summed)
        terms = ((count_b, ((0, 0), (1, 0))),)
        if own_a is not None:
            across_now = after(across, pair_sum)
            operands += (own_a, across_now, send(across_now, "rx", out_of))
            terms = ((count_a, ((2, 0), (3, 0), (4, 0))), *terms)
        if g + 1 < len(GROUPS):
            next_a, next_b = own[g + 1]
            along = send(after(next_b, pair_sum), "rx", into)
            across = None if next_a is None else send(after(next_a, summed), "rx", partner)
        total, pred, *tile = predict(0, inputs, operands, terms, (2, 3, 4) if g == 0 else ())
        if g == 0:
            (row_sum,) = tile
        mine, other = summed_over_ma(pred)
        if g + 1 < len(GROUPS):
            total = after(total, along, *([] if across is None else [across]))
        values, first_mid, second_mid = update_middle(
            rows[g], (inputs, targets, total, mine, other, row_sum, first, second), g == 0
        )
        ready = after(values, *results[-1][1:3]) if g > 0 else values
        results.append((values, *neighbours(ready, "ry"), first_mid, second_mid))

    outs = ()
    for batch in BATCHES:
        operands = []
        terms = []
        for g in batch:
            values, before, next_one = results[g][:3]
            values = after(values, results[-1][0], *([other] if outs else []))
            terms.append((sum(GROUPS[g]), tuple((len(operands) + i, 0) for i in range(3))))
            operands += [values, before, next_one]
        total, pred, *tile = predict(1, inputs, tuple(operands), tuple(terms), (0, 1, 2) if not outs else ())
        if not outs:
            (column_sum,) = tile
        mine, other = summed_over_ma(pred)
        moments = [block for g in batch for block in results[g][3:]]
        outs = update_last(
            rows[batch[0]],
            tuple((sum(GROUPS[g]), which, 0) for which, g in enumerate(batch)),
            (inputs, targets, total, mine, other, column_sum, *moments),
            numerator.shape,
            outs[:3],
        )
    new_numerator, new_first, new_second, new_weight = outs
    return new_numerator, new_weight, new_first, new_second


def solution(mesh):
    rows = P("rx", "ry", None, "ma")
    return jax.shard_map(
        local,
        mesh=mesh,
        in_specs=(
            rows,
            P("rx", "ry"),
            P("rx", "ry", None, None, "ma"),
            P("rx", "ry", None, None, None),
            rows,
            rows,
        ),
        out_specs=(rows, P("rx", "ry"), rows, rows),
        check_vma=False,
    )
```
